32 devices in a mesh: dp: 2 (over y), row: 4 (over x, core), col: 4 (over z).
Axes of the slice: x: 2, y: 2, z: 4, core: 2. Of those that a mesh axis runs over, the one named last changes fastest.
Arguments:
- tokens: bfloat16 [4096, 1024], P(('dp', 'row', 'col')), may hold values from -6 to 6
- cotangent: bfloat16 [4096, 1024], P(('dp', 'row', 'col')), may hold values from -6 to 6
- seq_lengths: int32 [8, 4], P(('dp', 'row')), may hold values from 1 to 384, 512 in all within a row
- routes: int32 [4096, 8], P(('dp', 'row', 'col')), may hold values from 0 to 31, all different within a row; in each aligned block of 128 rows (0 to 127, 128 to 255, ...) at most 34 rows name the same one
- gains: float32 [2, 1024], replicated, may hold values from 0.5 to 1.5
- gains_first: float32 [2, 1024], replicated, may hold values from -80 to 80
- gains_second: float32 [2, 1024], replicated, may hold values from 860.16 to 3440.64
- w_query: float32 [1024, 1024], P(('dp', 'row'), 'col'), may hold values from -0.1875 to 0.1875
- query_first: float32 [1024, 1024], P(('dp', 'row'), 'col'), may hold values from -80 to 80
- query_second: float32 [1024, 1024], P(('dp', 'row'), 'col'), may hold values from 860.16 to 3440.64
- w_key: float32 [1024, 512], P(('dp', 'row'), 'col'), may hold values from -0.1875 to 0.1875
- key_first: float32 [1024, 512], P(('dp', 'row'), 'col'), may hold values from -80 to 80
- key_second: float32 [1024, 512], P(('dp', 'row'), 'col'), may hold values from 860.16 to 3440.64
- w_value: float32 [1024, 512], P(('dp', 'row'), 'col'), may hold values from -0.1875 to 0.1875
- value_first: float32 [1024, 512], P(('dp', 'row'), 'col'), may hold values from -160 to 160
- value_second: float32 [1024, 512], P(('dp', 'row'), 'col'), may hold values from 3440.64 to 13926.4
- w_output: float32 [1024, 1024], P('col', ('dp', 'row')), may hold values from -0.75 to 0.75
- output_first: float32 [1024, 1024], P('col', ('dp', 'row')), may hold values from -32 to 32
- output_second: float32 [1024, 1024], P('col', ('dp', 'row')), may hold values from 139.264 to 552.96
- w_router: float32 [1024, 32], replicated, may hold values from -0.09375 to 0.09375
- router_first: float32 [1024, 32], replicated, may hold values from -128 to 128
- router_second: float32 [1024, 32], replicated, may hold values from 1925.12 to 7782.4
- w_gate: float32 [32, 1024, 512], P('dp', ('row', 'col')), may hold values from -0.1875 to 0.1875
- gate_first: float32 [32, 1024, 512], P('dp', ('row', 'col')), may hold values from -16 to 16
- gate_second: float32 [32, 1024, 512], P('dp', ('row', 'col')), may hold values from 34.4064 to 139.264
- w_up: float32 [32, 1024, 512], P('dp', ('row', 'col')), may hold values from -0.1875 to 0.1875
- up_first: float32 [32, 1024, 512], P('dp', ('row', 'col')), may hold values from -16 to 16
- up_second: float32 [32, 1024, 512], P('dp', ('row', 'col')), may hold values from 34.4064 to 139.264
- w_down: float32 [32, 512, 1024], P('dp', None, ('row', 'col')), may hold values from -1 to 1
- down_first: float32 [32, 512, 1024], P('dp', None, ('row', 'col')), may hold values from -3.5 to 3.5
- down_second: float32 [32, 512, 1024], P('dp', None, ('row', 'col')), may hold values from 1.39264 to 5.5296
Outputs:
- block_out: bfloat16 [4096, 1024], P(('dp', 'row', 'col'))
- tokens_grad: float32 [4096, 1024], P(('dp', 'row', 'col'))
- gains_new: float32 [2, 1024], replicated
- gains_first_new: float32 [2, 1024], replicated
- gains_second_new: float32 [2, 1024], replicated
- query_new: float32 [1024, 1024], P(('dp', 'row'), 'col')
- query_first_new: float32 [1024, 1024], P(('dp', 'row'), 'col')
- query_second_new: float32 [1024, 1024], P(('dp', 'row'), 'col')
- key_new: float32 [1024, 512], P(('dp', 'row'), 'col')
- key_first_new: float32 [1024, 512], P(('dp', 'row'), 'col')
- key_second_new: float32 [1024, 512], P(('dp', 'row'), 'col')
- value_new: float32 [1024, 512], P(('dp', 'row'), 'col')
- value_first_new: float32 [1024, 512], P(('dp', 'row'), 'col')
- value_second_new: float32 [1024, 512], P(('dp', 'row'), 'col')
- output_new: float32 [1024, 1024], P('col', ('dp', 'row'))
- output_first_new: float32 [1024, 1024], P('col', ('dp', 'row'))
- output_second_new: float32 [1024, 1024], P('col', ('dp', 'row'))
- router_new: float32 [1024, 32], replicated
- router_first_new: float32 [1024, 32], replicated
- router_second_new: float32 [1024, 32], replicated
- gate_new: float32 [32, 1024, 512], P('dp', ('row', 'col'))
- gate_first_new: float32 [32, 1024, 512], P('dp', ('row', 'col'))
- gate_second_new: float32 [32, 1024, 512], P('dp', ('row', 'col'))
- up_new: float32 [32, 1024, 512], P('dp', ('row', 'col'))
- up_first_new: float32 [32, 1024, 512], P('dp', ('row', 'col'))
- up_second_new: float32 [32, 1024, 512], P('dp', ('row', 'col'))
- down_new: float32 [32, 512, 1024], P('dp', None, ('row', 'col'))
- down_first_new: float32 [32, 512, 1024], P('dp', None, ('row', 'col'))
- down_second_new: float32 [32, 512, 1024], P('dp', None, ('row', 'col'))
The draws below stay inside these ranges and needn't reach their ends.
Inputs may be any that keep to these rules, and one draw needn't show every extreme that they name: `routes`: in each aligned block of 128 rows (the rows of one device) a row names 8 different experts, no expert is named by more than 34 rows, a bound that some block reaches; every expert is named somewhere. `seq_lengths`: each row sums to 512 and its largest entry is 384.
All inputs are finite; a program needn't handle non-finite values.
Results may differ from the reference program's by a relative error of at most 0.014.
Values may be sent and summed in bfloat16 or wider, within the bound.
A program may use at most 256 MiB of HBM per device.

```python
import math
import jax
import jax.numpy as jnp
import numpy as np
from jax import lax

D = 1024
QUERY_HEADS = 16
KEY_VALUE_HEADS = 8
HEAD_SIZE = 64
FF = 512
EXPERTS = 32
TOP = 8
TOK_DEV = 128
SEQS_BLOCK = 4
STEP = 10
Q_WIDTH = 1024
KEY_WIDTH = 512
TOKEN_TOTAL = 4096
ATTEND_ROW_COUNT = 512
ATT_BLOCKS = 8
MAX_LEN = 384
CAPACITY = 34


def block_scale(stream_key, dims, cuts, low, largest):
    gain = 1.0
    for dim, parts in cuts:
        heights = jax.random.uniform(jax.random.fold_in(jax.random.fold_in(stream_key, 6), dim), (parts,), jnp.float32, low / len(cuts), largest / len(cuts))
        gain = gain * jnp.repeat(jnp.exp(heights), dims[dim] // parts).reshape((-1,) + (1,) * (len(dims) - 1 - dim))
    return gain


def split_up(count, total, bound, lean):
    weights = [(1 << 20) // math.isqrt(standing ** lean) + 1 for standing in range(2, count + 1)]
    surplus, counts = total - bound - (count - 1), [1] * (count - 1)
    while surplus > 0:
        candidates = [i for i in range(count - 1) if counts[i] < bound]
        mass, left = sum([weights[i] for i in candidates]), surplus
        for i in candidates:
            addition = min(bound - counts[i], max(1, left * weights[i] // mass), surplus)
            counts[i] = counts[i] + addition
            surplus = surplus - addition
    return np.array([bound] + counts)


def ragged_sizes(rng, amount, total, bound, skew):
    if amount == 2:
        one = jax.random.randint(rng, (), max(1, total - bound), min(bound, total - 1) + 1)
        return jnp.stack([one, total - one])
    tallies = jnp.asarray(split_up(amount, total, bound, skew), jnp.int32)
    twos = (amount - 1) // 2
    giver, taker = tallies[1:1 + 2 * twos:2], tallies[2:2 + 2 * twos:2]
    margin = jnp.minimum(giver - 1, bound - taker)
    moved = jax.random.randint(jax.random.fold_in(rng, 1), (twos,), 0, 1 << 20) % (margin + 1)
    tallies = tallies.at[1:1 + 2 * twos:2].set(giver - moved).at[2:2 + 2 * twos:2].set(taker + moved)
    return tallies[jax.random.permutation(jax.random.fold_in(rng, 2), amount)]


def routed_block(stream_key, own, number, rows, amount, top, limit, skew):
    sequence = jax.random.permutation(stream_key, amount)
    crowded, common = load_shares(amount, rows * top, limit, skew, True), load_shares(amount, rows * top, limit, skew, False)
    places = jnp.arange(amount)

    def named(lengths, offset_by):
        used = int((lengths > 0).sum())
        fixed = max(1, used // 4)
        moved = fixed + (places - fixed + offset_by * (used - fixed)) % max(1, amount - fixed)
        return jnp.zeros((amount,), jnp.int32).at[sequence[jnp.where(places < fixed, places, moved)]].set(jnp.asarray(lengths, jnp.int32))

    lengths = jnp.where(number % 4 == 0, named(crowded, number // 4), named(common, number - number // 4 - 1))
    mixed = jax.random.permutation(jax.random.fold_in(own, 3), amount)
    giver, receiver = mixed[0:amount // 2 * 2:2], mixed[1:amount // 2 * 2:2]
    margin = jnp.minimum(lengths[giver] - 1, limit - lengths[receiver]) // 2
    margin = jnp.where((giver == sequence[0]) | (receiver == sequence[0]) | (lengths[receiver] == 0), 0, jnp.maximum(margin, 0))
    moved = jax.random.randint(jax.random.fold_in(own, 4), (amount // 2,), 0, 1 << 20) % (margin + 1)
    lengths = lengths.at[giver].add(-moved).at[receiver].add(moved)
    members = jnp.searchsorted(jnp.cumsum(lengths), jnp.arange(rows * top), side="right").astype(jnp.int32)
    grid = members.reshape(top, rows).T
    grid = grid[jax.random.permutation(jax.random.fold_in(own, 1), rows)]
    offset_by = jax.random.randint(jax.random.fold_in(own, 2), (rows, 1), 0, top)
    return jnp.take_along_axis(grid, (jnp.arange(top)[None, :] + offset_by) % top, axis=1)


def load_shares(amount, total, most, slope, full):
    weights = [(1 << 20) // math.isqrt(rank ** slope) + 1 for rank in range(1, amount + 1)]
    largest = most if full else min(most, max(-(-total // amount), total * weights[0] // sum(weights)))
    least = 1 if total - largest >= amount - 1 else 0
    holding, spare = [largest] + [least] * (amount - 1), total - largest - least * (amount - 1)
    while spare > 0:
        candidates = [i for i in range(1, amount) if holding[i] < largest] or [i for i in range(1, amount) if holding[i] < most]
        whole, remaining = sum([weights[i] for i in candidates]), spare
        for i in candidates:
            more = min(most - holding[i], max(1, remaining * weights[i] // whole), spare)
            holding[i] = holding[i] + more
            spare = spare - more
    return np.array(holding)


def scatter_about(key, shape, width, bound, split=(), held_as=jnp.bfloat16):
    drawn = width * jax.random.normal(key, shape, jnp.float32)
    if split:
        drawn = drawn * block_scale(key, shape, split, -0.22, 0.18)
    return jnp.clip(drawn, -bound, bound).astype(held_as)


def setup_inputs(seed: int = 0) -> dict:
    streams_of = jax.random.split(jax.random.key(seed), 32)
    tokens = scatter_about(streams_of[0], (TOKEN_TOTAL, D), 1.0, 6.0, ((0, 32),))
    cotangent = scatter_about(streams_of[1], (TOKEN_TOTAL, D), 1.0, 6.0, ((0, 32),))
    seq_lengths = jax.vmap(lambda own: ragged_sizes(own, SEQS_BLOCK, ATTEND_ROW_COUNT, MAX_LEN, 2))(jax.random.split(streams_of[2], ATT_BLOCKS)).reshape((ATT_BLOCKS, SEQS_BLOCK)).astype(jnp.int32)
    routes_keys = jax.random.split(jax.random.fold_in(streams_of[3], 1), TOKEN_TOTAL // TOK_DEV)
    routes_turns = jax.random.permutation(jax.random.fold_in(streams_of[3], 3), TOKEN_TOTAL // TOK_DEV)
    routes = jax.vmap(lambda own, number: routed_block(jax.random.fold_in(streams_of[3], 2), own, number, TOK_DEV, EXPERTS, TOP, CAPACITY, 1))(routes_keys, routes_turns).reshape((TOKEN_TOTAL, TOP))
    gains = jnp.clip(1.0 + 0.1 * jax.random.normal(streams_of[4], (2, D), jnp.float32), 0.5, 1.5)
    gains_first = scatter_about(streams_of[5], (2, D), (0.22 * TOKEN_TOTAL ** 0.5), 80.0, (), jnp.float32)
    gains_second = jnp.clip(jnp.exp(jax.random.uniform(streams_of[6], (2, D), jnp.float32, math.log(860.16), math.log(3440.64))), 860.16, 3440.64)
    w_query = scatter_about(streams_of[7], (D, Q_WIDTH), D ** -0.5, 0.1875, ((0, 8), (1, 4)), jnp.float32)
    query_first = scatter_about(streams_of[8], (D, Q_WIDTH), (0.22 * TOKEN_TOTAL ** 0.5), 80.0, ((0, 8), (1, 4)), jnp.float32)
    query_second = jnp.clip(jnp.exp(math.log(3440.64) - 1.3862944 * jax.random.uniform(streams_of[9], (D, Q_WIDTH), jnp.float32) ** block_scale(streams_of[9], (D, Q_WIDTH), ((0, 8), (1, 4)), -0.2, 0.2)), 860.16, 3440.64)
    w_key = scatter_about(streams_of[10], (D, KEY_WIDTH), D ** -0.5, 0.1875, ((0, 8), (1, 4)), jnp.float32)
    key_first = scatter_about(streams_of[11], (D, KEY_WIDTH), (0.22 * TOKEN_TOTAL ** 0.5), 80.0, ((0, 8), (1, 4)), jnp.float32)
    key_second = jnp.clip(jnp.exp(math.log(3440.64) - 1.3862944 * jax.random.uniform(streams_of[12], (D, KEY_WIDTH), jnp.float32) ** block_scale(streams_of[12], (D, KEY_WIDTH), ((0, 8), (1, 4)), -0.2, 0.2)), 860.16, 3440.64)
    w_value = scatter_about(streams_of[13], (D, KEY_WIDTH), D ** -0.5, 0.1875, ((0, 8), (1, 4)), jnp.float32)
    value_first = scatter_about(streams_of[14], (D, KEY_WIDTH), (0.44 * TOKEN_TOTAL ** 0.5), 160.0, ((0, 8), (1, 4)), jnp.float32)
    value_second = jnp.clip(jnp.exp(math.log(13926.4) - 1.3981289 * jax.random.uniform(streams_of[15], (D, KEY_WIDTH), jnp.float32) ** block_scale(streams_of[15], (D, KEY_WIDTH), ((0, 8), (1, 4)), -0.2, 0.2)), 3440.64, 13926.4)
    w_output = scatter_about(streams_of[16], (Q_WIDTH, D), (Q_WIDTH // 16) ** -0.5, 0.75, ((0, 4), (1, 8)), jnp.float32)
    output_first = scatter_about(streams_of[17], (Q_WIDTH, D), (0.089 * TOKEN_TOTAL ** 0.5), 32.0, ((0, 4), (1, 8)), jnp.float32)
    output_second = jnp.clip(jnp.exp(math.log(552.96) - 1.3789142 * jax.random.uniform(streams_of[18], (Q_WIDTH, D), jnp.float32) ** block_scale(streams_of[18], (Q_WIDTH, D), ((0, 4), (1, 8)), -0.2, 0.2)), 139.264, 552.96)
    w_router = scatter_about(streams_of[19], (D, EXPERTS), (4 * D) ** -0.5, 0.09375, (), jnp.float32)
    router_first = scatter_about(streams_of[20], (D, EXPERTS), (0.33 * TOKEN_TOTAL ** 0.5), 128.0, (), jnp.float32)
    router_second = jnp.clip(jnp.exp(jax.random.uniform(streams_of[21], (D, EXPERTS), jnp.float32, math.log(1925.12), math.log(7782.4))), 1925.12, 7782.4)
    w_gate = scatter_about(streams_of[22], (EXPERTS, D, FF), D ** -0.5, 0.1875, ((0, 2), (1, 16)), jnp.float32)
    gate_first = scatter_about(streams_of[23], (EXPERTS, D, FF), (0.044 * TOKEN_TOTAL ** 0.5), 16.0, ((0, 2), (1, 16)), jnp.float32)
    gate_second = jnp.clip(jnp.exp(math.log(139.264) - 1.3981289 * jax.random.uniform(streams_of[24], (EXPERTS, D, FF), jnp.float32) ** block_scale(streams_of[24], (EXPERTS, D, FF), ((0, 2), (1, 16)), -0.2, 0.2)), 34.4064, 139.264)
    w_up = scatter_about(streams_of[25], (EXPERTS, D, FF), D ** -0.5, 0.1875, ((0, 2), (1, 16)), jnp.float32)
    up_first = scatter_about(streams_of[26], (EXPERTS, D, FF), (0.044 * TOKEN_TOTAL ** 0.5), 16.0, ((0, 2), (1, 16)), jnp.float32)
    up_second = jnp.clip(jnp.exp(math.log(139.264) - 1.3981289 * jax.random.uniform(streams_of[27], (EXPERTS, D, FF), jnp.float32) ** block_scale(streams_of[27], (EXPERTS, D, FF), ((0, 2), (1, 16)), -0.2, 0.2)), 34.4064, 139.264)
    w_down = scatter_about(streams_of[28], (EXPERTS, FF, D), (FF // 16) ** -0.5, 1.0, ((0, 2), (2, 16)), jnp.float32)
    down_first = scatter_about(streams_of[29], (EXPERTS, FF, D), (0.0089 * TOKEN_TOTAL ** 0.5), 3.5, ((0, 2), (2, 16)), jnp.float32)
    down_second = jnp.clip(jnp.exp(math.log(5.5296) - 1.37891428 * jax.random.uniform(streams_of[30], (EXPERTS, FF, D), jnp.float32) ** block_scale(streams_of[30], (EXPERTS, FF, D), ((0, 2), (2, 16)), -0.2, 0.2)), 1.39264, 5.5296)
    return dict(tokens=tokens, cotangent=cotangent, seq_lengths=seq_lengths, routes=routes, gains=gains, gains_first=gains_first, gains_second=gains_second, w_query=w_query, query_first=query_first, query_second=query_second, w_key=w_key, key_first=key_first, key_second=key_second, w_value=w_value, value_first=value_first, value_second=value_second, w_output=w_output, output_first=output_first, output_second=output_second, w_router=w_router, router_first=router_first, router_second=router_second, w_gate=w_gate, gate_first=gate_first, gate_second=gate_second, w_up=w_up, up_first=up_first, up_second=up_second, w_down=w_down, down_first=down_first, down_second=down_second)


@jax.custom_vjp
def lower_precision(v):
    return lax.optimization_barrier(v.astype(jnp.bfloat16)).astype(jnp.float32)

@jax.custom_vjp
def low_back(v):
    return v

def low_keep(v):
    return (lower_precision(v), None)

def low_pass(kept, grad):
    return (grad,)

def back_keep(v):
    return (v, None)

def back_low(kept, grad):
    return (lower_precision(grad),)
lower_precision.defvjp(low_keep, low_pass)
low_back.defvjp(back_keep, back_low)
EPS_NORM = 1e-06
BETA_ONE = 0.9
BETA_TWO = 0.95
ADAM_EPS = 1e-08
WEIGHT_DECAY = 0.1
LEARN_RATE = 0.05
GAIN_RATE = 0.4
NEG_FILL = -1000000000.0
ROPE_BASE = 10000.0
PRECISE = lax.Precision.HIGHEST

def rms_norm(value_rows, gain_row):
    inverse = lax.rsqrt(lax.optimization_barrier(jnp.mean(value_rows * value_rows, axis=-1, keepdims=True)) + EPS_NORM)
    return value_rows * inverse * gain_row

def rope_tables(positions, head_dim):
    half_dim = head_dim // 2
    frequency = ROPE_BASE ** (-2.0 * jnp.arange(half_dim, dtype=jnp.float32) / head_dim)
    angles = positions[:, None] * frequency[None, :]
    return (jnp.cos(angles), jnp.sin(angles))

def apply_rotation(value_rows, cosine_lookup, sine_lookup):
    half_dim = value_rows.shape[-1] // 2
    first_half = value_rows[..., :half_dim]
    second_half = value_rows[..., half_dim:]
    cos_wide = cosine_lookup[:, None, :]
    sin_wide = sine_lookup[:, None, :]
    return jnp.concatenate([first_half * cos_wide - second_half * sin_wide, second_half * cos_wide + first_half * sin_wide], axis=-1)

def block_layout(lengths_row, row_count):
    seq_ends = jnp.cumsum(lengths_row).astype(jnp.int32)
    starts = seq_ends - lengths_row.astype(jnp.int32)
    row_index = jnp.arange(row_count, dtype=jnp.int32)
    member = (row_index[:, None] >= starts[None, :]) & (row_index[:, None] < seq_ends[None, :])
    numbers = jnp.arange(lengths_row.shape[0], dtype=jnp.int32)
    segment = lax.optimization_barrier(jnp.sum(jnp.where(member, numbers[None, :], 0), axis=1)).astype(jnp.int32)
    seq_begin = lax.optimization_barrier(jnp.sum(jnp.where(member, starts[None, :], 0), axis=1)).astype(jnp.int32)
    positions = (row_index - seq_begin).astype(jnp.float32)
    allowed = (segment[:, None] == segment[None, :]) & (row_index[None, :] <= row_index[:, None])
    return (positions, allowed)

def slot_tables(routes_rows, experts, capacity):
    copies = routes_rows.reshape(-1).astype(jnp.int32)
    copy_count = copies.shape[0]
    onehot = (copies[:, None] == jnp.arange(experts, dtype=jnp.int32)[None, :]).astype(jnp.int32)
    before = (jnp.cumsum(onehot, axis=0) - onehot).astype(jnp.int32)
    ranking = lax.optimization_barrier(jnp.sum(before * onehot, axis=1)).astype(jnp.int32)
    slot_of = copies * capacity + ranking
    slot_ids = jnp.arange(experts * capacity, dtype=jnp.int32)
    matches = slot_of[None, :] == slot_ids[:, None]
    filled = jnp.any(matches, axis=1)
    source = lax.optimization_barrier(jnp.sum(jnp.where(matches, jnp.arange(copy_count, dtype=jnp.int32)[None, :], 0), axis=1)).astype(jnp.int32)
    return (slot_of, source, filled)

def adam_update(weight, grad, first, second, rate, decay):
    first_new = BETA_ONE * first + (1.0 - BETA_ONE) * grad
    second_new = BETA_TWO * second + (1.0 - BETA_TWO) * grad * grad
    corr_one = 1.0 - BETA_ONE ** STEP
    corr_two = 1.0 - BETA_TWO ** STEP
    stepped = first_new / corr_one / (jnp.sqrt(second_new / corr_two) + ADAM_EPS)
    weight_new = weight - rate * (stepped + decay * weight)
    return (weight_new, first_new, second_new)

def attend_block(pieces):
    query_rows, key_rows, value_rows, allowed = pieces
    group_width = QUERY_HEADS // KEY_VALUE_HEADS
    query_rows_four = query_rows.reshape(ATTEND_ROW_COUNT, KEY_VALUE_HEADS, group_width, HEAD_SIZE)
    key_rows_three = key_rows.reshape(ATTEND_ROW_COUNT, KEY_VALUE_HEADS, HEAD_SIZE)
    value_rows_three = value_rows.reshape(ATTEND_ROW_COUNT, KEY_VALUE_HEADS, HEAD_SIZE)
    scores = jnp.einsum('qngd,knd->ngqk', query_rows_four, key_rows_three, precision=PRECISE) * HEAD_SIZE ** (-0.5)
    scores = low_back(scores)
    scores = jnp.where(allowed[None, None], scores, NEG_FILL)
    weights = jax.nn.softmax(scores, axis=-1)
    mixed = jnp.einsum('ngqk,knd->qngd', lower_precision(weights), value_rows_three, precision=PRECISE)
    return lower_precision(low_back(mixed.reshape(ATTEND_ROW_COUNT, Q_WIDTH)))

def expert_block(pieces, gate_low, up_low, down_low):
    normed, gates_rows, routes_rows = pieces
    slot_of, source, filled = slot_tables(routes_rows, EXPERTS, CAPACITY)
    source_token = source // TOP
    rows_in = jnp.where(filled[:, None], normed[source_token], 0.0)
    rows_in = low_back(rows_in).reshape(EXPERTS, CAPACITY, D)
    gate_pre = low_back(jnp.einsum('ecd,edf->ecf', rows_in, gate_low, precision=PRECISE))
    up_pre = low_back(jnp.einsum('ecd,edf->ecf', rows_in, up_low, precision=PRECISE))
    hidden_act = lower_precision(jax.nn.silu(gate_pre) * up_pre)
    result = lower_precision(low_back(jnp.einsum('ecf,efd->ecd', hidden_act, down_low, precision=PRECISE)))
    picked = result.reshape(EXPERTS * CAPACITY, D)[slot_of].reshape(TOK_DEV, TOP, D)
    return lax.optimization_barrier(jnp.sum(gates_rows[:, :, None] * picked, axis=1))

def forward(tokens_f, gains_v, wq, wk, wv, wo, wr, wg, wu, wd, positions, allowed, routes):
    normed_one = lower_precision(rms_norm(tokens_f, gains_v[0]))
    query_lin = low_back(jnp.dot(normed_one, lower_precision(wq), precision=PRECISE, preferred_element_type=jnp.float32))
    key_linear = low_back(jnp.dot(normed_one, lower_precision(wk), precision=PRECISE, preferred_element_type=jnp.float32))
    value_lin = jnp.dot(normed_one, lower_precision(wv), precision=PRECISE, preferred_element_type=jnp.float32)
    cosine_lookup, sine_lookup = rope_tables(positions, HEAD_SIZE)
    query_rows = lower_precision(apply_rotation(query_lin.reshape(TOKEN_TOTAL, QUERY_HEADS, HEAD_SIZE), cosine_lookup, sine_lookup).reshape(TOKEN_TOTAL, Q_WIDTH))
    key_rows = lower_precision(apply_rotation(key_linear.reshape(TOKEN_TOTAL, KEY_VALUE_HEADS, HEAD_SIZE), cosine_lookup, sine_lookup).reshape(TOKEN_TOTAL, KEY_WIDTH))
    value_rows = lower_precision(low_back(value_lin))
    mixed = lax.map(jax.checkpoint(attend_block), (query_rows.reshape(ATT_BLOCKS, ATTEND_ROW_COUNT, Q_WIDTH), key_rows.reshape(ATT_BLOCKS, ATTEND_ROW_COUNT, KEY_WIDTH), value_rows.reshape(ATT_BLOCKS, ATTEND_ROW_COUNT, KEY_WIDTH), allowed))
    attended = low_back(jnp.dot(mixed.reshape(TOKEN_TOTAL, Q_WIDTH), lower_precision(wo), precision=PRECISE, preferred_element_type=jnp.float32))
    hidden = tokens_f + attended
    normed_f = rms_norm(hidden, gains_v[1])
    normed_two = lower_precision(normed_f)
    logits = jnp.dot(normed_f, wr, precision=PRECISE, preferred_element_type=jnp.float32)
    chosen = jnp.take_along_axis(logits, routes, axis=1)
    gates = jax.nn.softmax(chosen, axis=-1)
    gate_low = lower_precision(wg)
    up_low = lower_precision(wu)
    down_low = lower_precision(wd)

    def run_block(pieces):
        return expert_block(pieces, gate_low, up_low, down_low)
    block_count = TOKEN_TOTAL // TOK_DEV
    moe = lax.map(jax.checkpoint(run_block), (normed_two.reshape(block_count, TOK_DEV, D), gates.reshape(block_count, TOK_DEV, TOP), routes.reshape(block_count, TOK_DEV, TOP)))
    return hidden + moe.reshape(TOKEN_TOTAL, D)

def reference(tokens, cotangent, seq_lengths, routes, gains, gains_first, gains_second, w_query, query_first, query_second, w_key, key_first, key_second, w_value, value_first, value_second, w_output, output_first, output_second, w_router, router_first, router_second, w_gate, gate_first, gate_second, w_up, up_first, up_second, w_down, down_first, down_second):

    def layout_row(lengths_row):
        return block_layout(lengths_row, ATTEND_ROW_COUNT)
    positions, allowed = jax.vmap(layout_row)(seq_lengths)
    positions = positions.reshape(TOKEN_TOTAL)
    routes_i = routes.astype(jnp.int32)

    def wrapped(tokens_f, gains_v, wq, wk, wv, wo, wr, wg, wu, wd):
        return forward(tokens_f, gains_v, wq, wk, wv, wo, wr, wg, wu, wd, positions, allowed, routes_i)
    block_f, pullback = jax.vjp(wrapped, tokens.astype(jnp.float32), gains, w_query, w_key, w_value, w_output, w_router, w_gate, w_up, w_down)
    grads = pullback(cotangent.astype(jnp.float32))
    tokens_grad, gains_g, query_g, key_g, value_g, output_g, router_g, gate_g, up_g, down_g = grads
    gains_out = adam_update(gains, gains_g, gains_first, gains_second, GAIN_RATE, 0.0)
    query_out = adam_update(w_query, query_g, query_first, query_second, LEARN_RATE, WEIGHT_DECAY)
    key_out = adam_update(w_key, key_g, key_first, key_second, LEARN_RATE, WEIGHT_DECAY)
    value_out = adam_update(w_value, value_g, value_first, value_second, LEARN_RATE, WEIGHT_DECAY)
    output_out = adam_update(w_output, output_g, output_first, output_second, LEARN_RATE, WEIGHT_DECAY)
    router_out = adam_update(w_router, router_g, router_first, router_second, LEARN_RATE, WEIGHT_DECAY)
    gate_out = adam_update(w_gate, gate_g, gate_first, gate_second, LEARN_RATE, WEIGHT_DECAY)
    up_out = adam_update(w_up, up_g, up_first, up_second, LEARN_RATE, WEIGHT_DECAY)
    down_out = adam_update(w_down, down_g, down_first, down_second, LEARN_RATE, WEIGHT_DECAY)
    return (block_f.astype(jnp.bfloat16), tokens_grad, gains_out[0], gains_out[1], gains_out[2], query_out[0], query_out[1], query_out[2], key_out[0], key_out[1], key_out[2], value_out[0], value_out[1], value_out[2], output_out[0], output_out[1], output_out[2], router_out[0], router_out[1], router_out[2], gate_out[0], gate_out[1], gate_out[2], up_out[0], up_out[1], up_out[2], down_out[0], down_out[1], down_out[2])
```

```python
import jax
import jax.numpy as jnp
from jax import lax
from jax.sharding import PartitionSpec as P

HEAD_SIZE = 64
EXPERTS = 32
STEP = 10
CAPACITY = 34


EPS_NORM = 1e-06
BETA_ONE = 0.9
BETA_TWO = 0.95
ADAM_EPS = 1e-08
WEIGHT_DECAY = 0.1
LEARN_RATE = 0.05
GAIN_RATE = 0.4
NEG_FILL = -1000000000.0
ROPE_BASE = 10000.0
PRECISE = lax.Precision.HIGHEST


def rope_tables(positions, head_dim):
    half_dim = head_dim // 2
    frequency = ROPE_BASE ** (-2.0 * jnp.arange(half_dim, dtype=jnp.float32) / head_dim)
    angles = positions[:, None] * frequency[None, :]
    return (jnp.cos(angles), jnp.sin(angles))


def apply_rotation(value_rows, cosine_lookup, sine_lookup):
    half_dim = value_rows.shape[-1] // 2
    first_half = value_rows[..., :half_dim]
    second_half = value_rows[..., half_dim:]
    cos_wide = cosine_lookup[:, None, :]
    sin_wide = sine_lookup[:, None, :]
    return jnp.concatenate(
        [
            first_half * cos_wide - second_half * sin_wide,
            second_half * cos_wide + first_half * sin_wide,
        ],
        axis=-1,
    )


def unrotate(value_rows, cosine_lookup, sine_lookup):
    half_dim = value_rows.shape[-1] // 2
    first_half = value_rows[..., :half_dim]
    second_half = value_rows[..., half_dim:]
    cos_wide = cosine_lookup[:, None, :]
    sin_wide = sine_lookup[:, None, :]
    return jnp.concatenate(
        [
            first_half * cos_wide + second_half * sin_wide,
            second_half * cos_wide - first_half * sin_wide,
        ],
        axis=-1,
    )


def block_layout(lengths_row, row_index):
    seq_ends = jnp.cumsum(lengths_row)
    starts = seq_ends - lengths_row
    member = (row_index[:, None] >= starts[None, :]) & (row_index[:, None] < seq_ends[None, :])
    numbers = jnp.arange(lengths_row.shape[0], dtype=jnp.int32)
    segment = jnp.sum(jnp.where(member, numbers[None, :], 0), axis=1)
    seq_begin = jnp.sum(jnp.where(member, starts[None, :], 0), axis=1)
    positions = (row_index - seq_begin).astype(jnp.float32)
    allowed = (segment[:, None] == segment[None, :]) & (row_index[None, :] <= row_index[:, None])
    return (positions, allowed)


def adam_update(weight, grad, first, second, rate, decay):
    first_new = BETA_ONE * first + (1.0 - BETA_ONE) * grad
    second_new = BETA_TWO * second + (1.0 - BETA_TWO) * grad * grad
    corr_one = 1.0 - BETA_ONE**STEP
    corr_two = 1.0 - BETA_TWO**STEP
    stepped = first_new / corr_one / (jnp.sqrt(second_new / corr_two) + ADAM_EPS)
    weight_new = weight - rate * (stepped + decay * weight)
    return (weight_new, first_new, second_new)


def norm_back(value_rows, inverse, gain_row, upstream):
    scaled = upstream * gain_row
    inner = jnp.mean(scaled * value_rows, axis=-1, keepdims=True)
    grad_in = inverse * scaled - value_rows * inverse * inverse * inverse * inner
    grad_gain = jnp.sum(upstream * value_rows * inverse, axis=0)
    return (grad_in, grad_gain)


def contract_rows(left, right):
    return lax.dot_general(
        left, right, (((0,), (0,)), ((), ())), preferred_element_type=jnp.float32
    )


def contract_cols(left, right):
    return lax.dot_general(
        left, right, (((1,), (1,)), ((), ())), preferred_element_type=jnp.float32
    )


def masked_scores(query_b, keys_b, allowed, scale_factor):
    raw = (
        jnp.einsum("qngd,knd->ngqk", query_b, keys_b, preferred_element_type=jnp.float32)
        * scale_factor
    )
    return jnp.where(allowed[None, None], raw, NEG_FILL)


def partner_list(axis, step):
    return [(i, i ^ step) for i in range(lax.axis_size(axis))]


def gather_partners(rows, axis):
    pieces = [rows]
    for step in range(1, lax.axis_size(axis)):
        pieces.append(lax.ppermute(rows, axis, partner_list(axis, step)))
    return jnp.concatenate(pieces, axis=0)


def sum_partners(partial_rows, axis, rows):
    total = partial_rows[:rows].astype(jnp.float32)
    for step in range(1, lax.axis_size(axis)):
        share = partial_rows[step * rows : (step + 1) * rows].astype(jnp.bfloat16)
        share = lax.ppermute(share, axis, partner_list(axis, step))
        total = total + share.astype(jnp.float32)
    return total


def exchange_sum(partial_rows, axes, count):
    rows, columns = partial_rows.shape
    shares = lax.all_to_all(
        partial_rows.reshape(count, rows // count, columns),
        axes,
        split_axis=0,
        concat_axis=0,
        tiled=True,
    )
    return jnp.sum(shares.astype(jnp.float32), axis=0)


def sum_all(values, axes):
    for axis in axes:
        count = lax.axis_size(axis)
        if count & (count - 1):
            values = lax.psum(values, axis)
            continue
        step = 1
        while step < count:
            partners = [(i, i ^ step) for i in range(count)]
            values = values + lax.ppermute(values, axis, partners)
            step *= 2
    return values


def on_device(
    tokens,
    cotangent,
    seq_lengths,
    routes,
    gains,
    gains_first,
    gains_second,
    w_query,
    query_first,
    query_second,
    w_key,
    key_first,
    key_second,
    w_value,
    value_first,
    value_second,
    w_output,
    output_first,
    output_second,
    w_router,
    router_first,
    router_second,
    w_gate,
    gate_first,
    gate_second,
    w_up,
    up_first,
    up_second,
    w_down,
    down_first,
    down_second,
):
    bf16 = jnp.bfloat16
    f32 = jnp.float32
    dp_count = lax.axis_size("dp")
    col_count = lax.axis_size("col")
    owner_count = dp_count * lax.axis_size("row")
    group_count = lax.axis_size("row") * col_count
    tok_rows = tokens.shape[0]
    width = tokens.shape[1]
    local_experts = EXPERTS // dp_count
    ff = w_gate.shape[2]
    whole_experts = local_experts == group_count
    expert_axes = ("dp", "row", "col") if whole_experts else ("dp",)
    sources = EXPERTS if whole_experts else dp_count
    held_experts = EXPERTS // sources

    q_cols = w_query.shape[1]
    kv_cols = w_key.shape[1]
    joint_cols = q_cols + 2 * kv_cols
    attention_w = lax.all_gather(
        jnp.concatenate([w_query, w_key, w_value, w_output.T], axis=1).astype(bf16),
        ("dp", "row"),
        axis=0,
        tiled=True,
    )
    joint_w = attention_w[:, :joint_cols]
    output_wt = attention_w[:, joint_cols:]
    tokens_f = tokens.astype(f32)
    inverse_one = lax.rsqrt(jnp.mean(tokens_f * tokens_f, axis=-1, keepdims=True) + EPS_NORM)
    normed_one = (tokens_f * inverse_one * gains[0]).astype(bf16)
    block_rows = gather_partners(normed_one, "col")

    expert_w = jnp.concatenate(
        [w_gate.astype(bf16), w_up.astype(bf16), jnp.swapaxes(w_down.astype(bf16), 1, 2)], axis=2
    )
    if whole_experts:
        expert_w = lax.all_to_all(
            expert_w, ("row", "col"), split_axis=0, concat_axis=0, tiled=True
        ).reshape(1, width, 3 * ff)
    else:
        expert_w = lax.all_gather(expert_w, ("row", "col"), axis=1, tiled=True)
    in_w = expert_w[:, :, : 2 * ff]
    down_wt = expert_w[:, :, 2 * ff :]

    heads_q = q_cols // HEAD_SIZE
    heads_kv = kv_cols // HEAD_SIZE
    group_width = heads_q // heads_kv
    scale_factor = HEAD_SIZE ** (-0.5)
    projected = jnp.dot(block_rows, joint_w, preferred_element_type=f32)
    att_rows = projected.shape[0]
    turned = jnp.arange(col_count, dtype=jnp.int32) ^ lax.axis_index("col")
    row_index = (turned[:, None] * tok_rows + jnp.arange(tok_rows, dtype=jnp.int32)).reshape(-1)
    positions, allowed = block_layout(seq_lengths[0], row_index)
    cosine_lookup, sine_lookup = rope_tables(positions, HEAD_SIZE)
    query_lin = projected[:, :q_cols].reshape(att_rows, heads_q, HEAD_SIZE)
    key_linear = projected[:, q_cols : q_cols + kv_cols].reshape(att_rows, heads_kv, HEAD_SIZE)
    value_lin = projected[:, q_cols + kv_cols :]
    query_b = (
        apply_rotation(query_lin, cosine_lookup, sine_lookup)
        .astype(bf16)
        .reshape(att_rows, heads_kv, group_width, HEAD_SIZE)
    )
    keys_b = apply_rotation(key_linear, cosine_lookup, sine_lookup).astype(bf16)
    values_b = value_lin.astype(bf16).reshape(att_rows, heads_kv, HEAD_SIZE)
    scores = masked_scores(query_b, keys_b, allowed, scale_factor)
    peak = jnp.max(scores, axis=-1, keepdims=True)
    expo = jnp.exp(scores - peak)
    total = jnp.sum(expo, axis=-1, keepdims=True)
    probs = expo / total
    log_total = peak + jnp.log(total)
    mixed_b = (
        jnp.einsum("ngqk,knd->qngd", probs.astype(bf16), values_b, preferred_element_type=f32)
        .astype(bf16)
        .reshape(att_rows, q_cols)
    )
    attended = sum_partners(contract_cols(mixed_b, output_wt), "col", tok_rows)
    hidden = tokens_f + attended
    inverse_two = lax.rsqrt(jnp.mean(hidden * hidden, axis=-1, keepdims=True) + EPS_NORM)
    normed_f = hidden * inverse_two * gains[1]
    normed_two = normed_f.astype(bf16)
    logits = jnp.dot(normed_f, w_router, precision=PRECISE, preferred_element_type=f32)

    expert_ids = jnp.arange(EXPERTS, dtype=jnp.int32)
    chosen = jnp.any(routes[:, :, None] == expert_ids[None, None, :], axis=1)
    earlier = jnp.tril(jnp.ones((tok_rows, tok_rows), bf16), -1)
    ranking = jnp.dot(earlier, chosen.astype(bf16), preferred_element_type=f32).astype(jnp.int32)
    rank_of = jnp.where(chosen, ranking, -1).T
    slot_ids = jnp.arange(CAPACITY, dtype=jnp.int32)
    in_slot = rank_of[:, None, :] == slot_ids[None, :, None]
    slot_count = EXPERTS * CAPACITY
    pick = in_slot.astype(bf16).reshape(slot_count, tok_rows)

    masked_logits = jnp.where(chosen, logits, NEG_FILL)
    gate_exp = jnp.where(
        chosen, jnp.exp(masked_logits - jnp.max(masked_logits, axis=-1, keepdims=True)), 0.0
    )
    gates = gate_exp / jnp.sum(gate_exp, axis=-1, keepdims=True)
    gates_t = gates.T
    slot_gates = jnp.where(in_slot, gates_t[:, None, :], 0.0)
    slot_gate = jnp.sum(slot_gates, axis=-1).reshape(slot_count, 1)
    slot_gates = slot_gates.reshape(slot_count, tok_rows)
    gates_high = slot_gates.astype(bf16)
    gates_low = (slot_gates - gates_high.astype(f32)).astype(bf16)

    def dispatch(first_rows, second_rows):
        slots = (sources, held_experts, CAPACITY, width)
        both = jnp.concatenate([first_rows.reshape(slots), second_rows.reshape(slots)], axis=2)
        moved = lax.all_to_all(both, expert_axes, split_axis=0, concat_axis=0, tiled=True)
        moved = jnp.swapaxes(moved, 0, 1)
        held = (held_experts, sources * CAPACITY, width)
        return (moved[:, :, :CAPACITY].reshape(held), moved[:, :, CAPACITY:].reshape(held))

    def bring_back(first_rows, second_rows):
        held = (held_experts, sources, CAPACITY, width)
        both = jnp.concatenate([first_rows.reshape(held), second_rows.reshape(held)], axis=2)
        moved = lax.all_to_all(
            jnp.swapaxes(both, 0, 1), expert_axes, split_axis=0, concat_axis=0, tiled=True
        )
        slots = (slot_count, width)
        return (
            moved[:, :, :CAPACITY].reshape(slots),
            moved[:, :, CAPACITY:].reshape(slots),
        )

    upstream = cotangent.astype(f32)
    received, received_grad = dispatch(
        jnp.dot(pick, normed_two, preferred_element_type=f32).astype(bf16),
        (slot_gate * jnp.dot(pick, cotangent, preferred_element_type=f32)).astype(bf16),
    )
    pre = jnp.einsum("jrd,jdf->jrf", received, in_w, preferred_element_type=f32)
    gate_pre = pre[:, :, :ff]
    up_pre = pre[:, :, ff:]
    sigm = jax.nn.sigmoid(gate_pre)
    silu_gate = gate_pre * sigm
    hidden_act = (silu_gate * up_pre).astype(bf16)
    act_grad = jnp.einsum("jrd,jdf->jrf", received_grad, down_wt, preferred_element_type=f32)
    silu_slope = sigm * (1.0 + gate_pre * (1.0 - sigm))
    pre_grad = jnp.concatenate(
        [(act_grad * up_pre * silu_slope).astype(bf16), (act_grad * silu_gate).astype(bf16)],
        axis=2,
    )
    returned, returned_grad = bring_back(
        jnp.einsum("jrf,jdf->jrd", hidden_act, down_wt, preferred_element_type=f32).astype(bf16),
        jnp.einsum("jrf,jdf->jrd", pre_grad, in_w, preferred_element_type=f32).astype(bf16),
    )
    in_wgrad = jnp.einsum("jrd,jrf->jdf", received, pre_grad, preferred_element_type=f32)
    down_wtgrad = jnp.einsum(
        "jrd,jrf->jdf", received_grad, hidden_act, preferred_element_type=f32
    )
    expert_wgrad = jnp.concatenate([in_wgrad.astype(bf16), down_wtgrad.astype(bf16)], axis=2)

    moe = contract_rows(gates_high, returned) + contract_rows(gates_low, returned)
    block_out = (hidden + moe).astype(bf16)
    all_gate_grads = contract_cols(returned, cotangent).reshape(EXPERTS, CAPACITY, tok_rows)
    gate_grads = jnp.sum(jnp.where(in_slot, all_gate_grads, 0.0), axis=1).T
    logit_grad = gates * (gate_grads - jnp.sum(gates * gate_grads, axis=-1, keepdims=True))
    router_grad_t = lax.dot_general(
        logit_grad,
        normed_f,
        (((0,), (0,)), ((), ())),
        precision=PRECISE,
        preferred_element_type=f32,
    )
    normed_grad = lax.dot_general(
        logit_grad,
        w_router,
        (((1,), (1,)), ((), ())),
        precision=PRECISE,
        preferred_element_type=f32,
    ) + contract_rows(pick, returned_grad)
    hidden_norm_grad, gain_two_grad = norm_back(hidden, inverse_two, gains[1], normed_grad)
    hidden_grad = upstream + hidden_norm_grad
    attended_grad = hidden_grad.astype(bf16)
    piece = gather_partners(attended_grad, "col")
    part = jnp.dot(piece, output_wt, preferred_element_type=f32)
    output_wtgrad = contract_rows(piece, mixed_b)
    mixed_grad_b = part.astype(bf16).reshape(att_rows, heads_kv, group_width, HEAD_SIZE)
    scores_again = masked_scores(query_b, keys_b, allowed, scale_factor)
    probs_again = jnp.exp(scores_again - log_total)
    probs_grad = jnp.einsum("qngd,knd->ngqk", mixed_grad_b, values_b, preferred_element_type=f32)
    value_grad = jnp.einsum(
        "ngqk,qngd->knd", probs_again.astype(bf16), mixed_grad_b, preferred_element_type=f32
    )
    inner_sum = jnp.sum(probs_again * probs_grad, axis=-1, keepdims=True)
    score_grad = (probs_again * (probs_grad - inner_sum)).astype(bf16)
    query_grad = (
        jnp.einsum("ngqk,knd->qngd", score_grad, keys_b, preferred_element_type=f32) * scale_factor
    )
    key_grad = (
        jnp.einsum("ngqk,qngd->knd", score_grad, query_b, preferred_element_type=f32) * scale_factor
    )
    query_lin_grad = (
        unrotate(query_grad.reshape(att_rows, heads_q, HEAD_SIZE), cosine_lookup, sine_lookup)
        .astype(bf16)
        .reshape(att_rows, q_cols)
    )
    key_lin_grad = (
        unrotate(key_grad, cosine_lookup, sine_lookup).astype(bf16).reshape(att_rows, kv_cols)
    )
    value_lin_grad = value_grad.astype(bf16).reshape(att_rows, kv_cols)
    joint_grad = jnp.concatenate([query_lin_grad, key_lin_grad, value_lin_grad], axis=1)
    normed_one_grad = sum_partners(contract_cols(joint_grad, joint_w), "col", tok_rows)
    joint_wgrad = contract_rows(block_rows, joint_grad)
    tokens_norm_grad, gain_one_grad = norm_back(tokens_f, inverse_one, gains[0], normed_one_grad)
    tokens_grad = hidden_grad + tokens_norm_grad

    attention_g = exchange_sum(
        jnp.concatenate([joint_wgrad.astype(bf16), output_wtgrad.astype(bf16)], axis=1),
        ("dp", "row"),
        owner_count,
    )
    query_g = attention_g[:, :q_cols]
    key_g = attention_g[:, q_cols : q_cols + kv_cols]
    value_g = attention_g[:, q_cols + kv_cols : joint_cols]
    output_g = attention_g[:, joint_cols:].T
    if whole_experts:
        expert_g = lax.all_to_all(
            expert_wgrad.reshape(group_count, width // group_count, 3 * ff),
            ("row", "col"),
            split_axis=0,
            concat_axis=0,
            tiled=True,
        ).astype(f32)
    else:
        expert_g = lax.psum_scatter(
            expert_wgrad, ("row", "col"), scatter_dimension=1, tiled=True
        ).astype(f32)
    gate_g = expert_g[:, :, :ff]
    up_g = expert_g[:, :, ff : 2 * ff]
    down_g = jnp.swapaxes(expert_g[:, :, 2 * ff :], 1, 2)
    small_total = sum_all(
        jnp.concatenate([gain_one_grad[None], gain_two_grad[None], router_grad_t], axis=0),
        ("dp", "row", "col"),
    )
    gains_total = small_total[:2]
    router_total = small_total[2:].T
    gains_out = adam_update(gains, gains_total, gains_first, gains_second, GAIN_RATE, 0.0)
    query_out = adam_update(w_query, query_g, query_first, query_second, LEARN_RATE, WEIGHT_DECAY)
    key_out = adam_update(w_key, key_g, key_first, key_second, LEARN_RATE, WEIGHT_DECAY)
    value_out = adam_update(w_value, value_g, value_first, value_second, LEARN_RATE, WEIGHT_DECAY)
    output_out = adam_update(
        w_output, output_g, output_first, output_second, LEARN_RATE, WEIGHT_DECAY
    )
    router_out = adam_update(
        w_router, router_total, router_first, router_second, LEARN_RATE, WEIGHT_DECAY
    )
    gate_out = adam_update(w_gate, gate_g, gate_first, gate_second, LEARN_RATE, WEIGHT_DECAY)
    up_out = adam_update(w_up, up_g, up_first, up_second, LEARN_RATE, WEIGHT_DECAY)
    down_out = adam_update(w_down, down_g, down_first, down_second, LEARN_RATE, WEIGHT_DECAY)
    return (
        block_out,
        tokens_grad,
        gains_out[0],
        gains_out[1],
        gains_out[2],
        query_out[0],
        query_out[1],
        query_out[2],
        key_out[0],
        key_out[1],
        key_out[2],
        value_out[0],
        value_out[1],
        value_out[2],
        output_out[0],
        output_out[1],
        output_out[2],
        router_out[0],
        router_out[1],
        router_out[2],
        gate_out[0],
        gate_out[1],
        gate_out[2],
        up_out[0],
        up_out[1],
        up_out[2],
        down_out[0],
        down_out[1],
        down_out[2],
    )


def solution(mesh):
    placed = (
        P(("dp", "row", "col"), None),
        P(("dp", "row", "col"), None),
        P(("dp", "row"), None),
        P(("dp", "row", "col"), None),
        P(),
        P(),
        P(),
        P(("dp", "row"), "col"),
        P(("dp", "row"), "col"),
        P(("dp", "row"), "col"),
        P(("dp", "row"), "col"),
        P(("dp", "row"), "col"),
        P(("dp", "row"), "col"),
        P(("dp", "row"), "col"),
        P(("dp", "row"), "col"),
        P(("dp", "row"), "col"),
        P("col", ("dp", "row")),
        P("col", ("dp", "row")),
        P("col", ("dp", "row")),
        P(),
        P(),
        P(),
        P("dp", ("row", "col"), None),
        P("dp", ("row", "col"), None),
        P("dp", ("row", "col"), None),
        P("dp", ("row", "col"), None),
        P("dp", ("row", "col"), None),
        P("dp", ("row", "col"), None),
        P("dp", None, ("row", "col")),
        P("dp", None, ("row", "col")),
        P("dp", None, ("row", "col")),
    )
    return jax.shard_map(
        on_device,
        mesh=mesh,
        in_specs=placed,
        out_specs=(
            P(("dp", "row", "col"), None),
            P(("dp", "row", "col"), None),
            P(),
            P(),
            P(),
            P(("dp", "row"), "col"),
            P(("dp", "row"), "col"),
            P(("dp", "row"), "col"),
            P(("dp", "row"), "col"),
            P(("dp", "row"), "col"),
            P(("dp", "row"), "col"),
            P(("dp", "row"), "col"),
            P(("dp", "row"), "col"),
            P(("dp", "row"), "col"),
            P("col", ("dp", "row")),
            P("col", ("dp", "row")),
            P("col", ("dp", "row")),
            P(),
            P(),
            P(),
            P("dp", ("row", "col"), None),
            P("dp", ("row", "col"), None),
            P("dp", ("row", "col"), None),
            P("dp", ("row", "col"), None),
            P("dp", ("row", "col"), None),
            P("dp", ("row", "col"), None),
            P("dp", None, ("row", "col")),
            P("dp", None, ("row", "col")),
            P("dp", None, ("row", "col")),
        ),
        check_vma=False,
    )
```

```python
import jax
import jax.numpy as jnp
from jax import lax
from jax.sharding import PartitionSpec as P

HEAD_SIZE = 64
EXPERTS = 32
STEP = 10
CAPACITY = 34


EPS_NORM = 1e-06
BETA_ONE = 0.9
BETA_TWO = 0.95
ADAM_EPS = 1e-08
WEIGHT_DECAY = 0.1
LEARN_RATE = 0.05
GAIN_RATE = 0.4
NEG_FILL = -1000000000.0
ROPE_BASE = 10000.0
PRECISE = lax.Precision.HIGHEST


def rope_tables(positions, head_dim):
    half_dim = head_dim // 2
    frequency = ROPE_BASE ** (-2.0 * jnp.arange(half_dim, dtype=jnp.float32) / head_dim)
    angles = positions[:, None] * frequency[None, :]
    return (jnp.cos(angles), jnp.sin(angles))


def apply_rotation(value_rows, cosine_lookup, sine_lookup):
    half_dim = value_rows.shape[-1] // 2
    first_half = value_rows[..., :half_dim]
    second_half = value_rows[..., half_dim:]
    cos_wide = cosine_lookup[:, None, :]
    sin_wide = sine_lookup[:, None, :]
    return jnp.concatenate(
        [
            first_half * cos_wide - second_half * sin_wide,
            second_half * cos_wide + first_half * sin_wide,
        ],
        axis=-1,
    )


def unrotate(value_rows, cosine_lookup, sine_lookup):
    half_dim = value_rows.shape[-1] // 2
    first_half = value_rows[..., :half_dim]
    second_half = value_rows[..., half_dim:]
    cos_wide = cosine_lookup[:, None, :]
    sin_wide = sine_lookup[:, None, :]
    return jnp.concatenate(
        [
            first_half * cos_wide + second_half * sin_wide,
            second_half * cos_wide - first_half * sin_wide,
        ],
        axis=-1,
    )


def block_layout(lengths_row, row_index):
    seq_ends = jnp.cumsum(lengths_row)
    starts = seq_ends - lengths_row
    member = (row_index[:, None] >= starts[None, :]) & (row_index[:, None] < seq_ends[None, :])
    numbers = jnp.arange(lengths_row.shape[0], dtype=jnp.int32)
    segment = jnp.sum(jnp.where(member, numbers[None, :], 0), axis=1)
    seq_begin = jnp.sum(jnp.where(member, starts[None, :], 0), axis=1)
    positions = (row_index - seq_begin).astype(jnp.float32)
    allowed = (segment[:, None] == segment[None, :]) & (row_index[None, :] <= row_index[:, None])
    return (positions, allowed)


def adam_update(weight, grad, first, second, rate, decay):
    first_new = BETA_ONE * first + (1.0 - BETA_ONE) * grad
    second_new = BETA_TWO * second + (1.0 - BETA_TWO) * grad * grad
    corr_one = 1.0 - BETA_ONE**STEP
    corr_two = 1.0 - BETA_TWO**STEP
    stepped = first_new / corr_one / (jnp.sqrt(second_new / corr_two) + ADAM_EPS)
    weight_new = weight - rate * (stepped + decay * weight)
    return (weight_new, first_new, second_new)


def norm_back(value_rows, inverse, gain_row, upstream):
    scaled = upstream * gain_row
    inner = jnp.mean(scaled * value_rows, axis=-1, keepdims=True)
    grad_in = inverse * scaled - value_rows * inverse * inverse * inverse * inner
    grad_gain = jnp.sum(upstream * value_rows * inverse, axis=0)
    return (grad_in, grad_gain)


def contract_rows(left, right):
    return lax.dot_general(
        left, right, (((0,), (0,)), ((), ())), preferred_element_type=jnp.float32
    )


def contract_cols(left, right):
    return lax.dot_general(
        left, right, (((1,), (1,)), ((), ())), preferred_element_type=jnp.float32
    )


def masked_scores(query_b, keys_b, allowed, scale_factor):
    raw = (
        jnp.einsum("qngd,knd->ngqk", query_b, keys_b, preferred_element_type=jnp.float32)
        * scale_factor
    )
    return jnp.where(allowed[None, None], raw, NEG_FILL)


def partner_list(axis, step):
    return [(i, i ^ step) for i in range(lax.axis_size(axis))]


def gather_partners(rows, axis):
    pieces = [rows]
    for step in range(1, lax.axis_size(axis)):
        pieces.append(lax.ppermute(rows, axis, partner_list(axis, step)))
    return jnp.concatenate(pieces, axis=0)


def sum_partners(partial_rows, axis, rows):
    total = partial_rows[:rows].astype(jnp.float32)
    for step in range(1, lax.axis_size(axis)):
        share = partial_rows[step * rows : (step + 1) * rows].astype(jnp.bfloat16)
        share = lax.ppermute(share, axis, partner_list(axis, step))
        total = total + share.astype(jnp.float32)
    return total


def exchange_sum(partial_rows, axes, count):
    rows, columns = partial_rows.shape
    shares = lax.all_to_all(
        partial_rows.reshape(count, rows // count, columns),
        axes,
        split_axis=0,
        concat_axis=0,
        tiled=True,
    )
    return jnp.sum(shares.astype(jnp.float32), axis=0)


def sum_all(values, axes):
    for axis in axes:
        count = lax.axis_size(axis)
        if count & (count - 1):
            values = lax.psum(values, axis)
            continue
        step = 1
        while step < count:
            partners = [(i, i ^ step) for i in range(count)]
            values = values + lax.ppermute(values, axis, partners)
            step *= 2
    return values


def on_device(
    tokens,
    cotangent,
    seq_lengths,
    routes,
    gains,
    gains_first,
    gains_second,
    w_query,
    query_first,
    query_second,
    w_key,
    key_first,
    key_second,
    w_value,
    value_first,
    value_second,
    w_output,
    output_first,
    output_second,
    w_router,
    router_first,
    router_second,
    w_gate,
    gate_first,
    gate_second,
    w_up,
    up_first,
    up_second,
    w_down,
    down_first,
    down_second,
):
    bf16 = jnp.bfloat16
    f32 = jnp.float32
    dp_count = lax.axis_size("dp")
    col_count = lax.axis_size("col")
    owner_count = dp_count * lax.axis_size("row")
    group_count = lax.axis_size("row") * col_count
    tok_rows = tokens.shape[0]
    width = tokens.shape[1]
    local_experts = EXPERTS // dp_count
    ff = w_gate.shape[2]
    whole_experts = local_experts == group_count
    expert_axes = ("dp", "row") if whole_experts else ("dp",)
    share_count = col_count if whole_experts else 1
    near_experts = EXPERTS // share_count
    sources = owner_count if whole_experts else dp_count
    held_experts = near_experts // sources
    slot_rows = CAPACITY * share_count

    q_cols = w_query.shape[1]
    kv_cols = w_key.shape[1]
    joint_cols = q_cols + 2 * kv_cols
    attention_w = lax.all_gather(
        jnp.concatenate([w_query, w_key, w_value, w_output.T], axis=1).astype(bf16),
        ("dp", "row"),
        axis=0,
        tiled=True,
    )
    joint_w = attention_w[:, :joint_cols]
    output_wt = attention_w[:, joint_cols:]
    tokens_f = tokens.astype(f32)
    inverse_one = lax.rsqrt(jnp.mean(tokens_f * tokens_f, axis=-1, keepdims=True) + EPS_NORM)
    normed_one = (tokens_f * inverse_one * gains[0]).astype(bf16)
    block_rows = gather_partners(normed_one, "col")

    expert_w = jnp.concatenate(
        [w_gate.astype(bf16), w_up.astype(bf16), jnp.swapaxes(w_down.astype(bf16), 1, 2)], axis=2
    )
    if whole_experts:
        expert_w = lax.all_to_all(
            expert_w, ("row", "col"), split_axis=0, concat_axis=0, tiled=True
        ).reshape(1, width, 3 * ff)
    else:
        expert_w = lax.all_gather(expert_w, ("row", "col"), axis=1, tiled=True)
    heads_q = q_cols // HEAD_SIZE
    heads_kv = kv_cols // HEAD_SIZE
    group_width = heads_q // heads_kv
    scale_factor = HEAD_SIZE ** (-0.5)
    projected = jnp.dot(block_rows, joint_w, preferred_element_type=f32)
    att_rows = projected.shape[0]
    turned = jnp.arange(col_count, dtype=jnp.int32) ^ lax.axis_index("col")
    row_index = (turned[:, None] * tok_rows + jnp.arange(tok_rows, dtype=jnp.int32)).reshape(-1)
    positions, allowed = block_layout(seq_lengths[0], row_index)
    cosine_lookup, sine_lookup = rope_tables(positions, HEAD_SIZE)
    query_lin = projected[:, :q_cols].reshape(att_rows, heads_q, HEAD_SIZE)
    key_linear = projected[:, q_cols : q_cols + kv_cols].reshape(att_rows, heads_kv, HEAD_SIZE)
    value_lin = projected[:, q_cols + kv_cols :]
    query_b = (
        apply_rotation(query_lin, cosine_lookup, sine_lookup)
        .astype(bf16)
        .reshape(att_rows, heads_kv, group_width, HEAD_SIZE)
    )
    keys_b = apply_rotation(key_linear, cosine_lookup, sine_lookup).astype(bf16)
    values_b = value_lin.astype(bf16).reshape(att_rows, heads_kv, HEAD_SIZE)
    scores = masked_scores(query_b, keys_b, allowed, scale_factor)
    peak = jnp.max(scores, axis=-1, keepdims=True)
    expo = jnp.exp(scores - peak)
    total = jnp.sum(expo, axis=-1, keepdims=True)
    probs = expo / total
    log_total = peak + jnp.log(total)
    mixed_b = (
        jnp.einsum("ngqk,knd->qngd", probs.astype(bf16), values_b, preferred_element_type=f32)
        .astype(bf16)
        .reshape(att_rows, q_cols)
    )
    attended = sum_partners(contract_cols(mixed_b, output_wt), "col", tok_rows)
    hidden = tokens_f + attended
    inverse_two = lax.rsqrt(jnp.mean(hidden * hidden, axis=-1, keepdims=True) + EPS_NORM)
    normed_f = hidden * inverse_two * gains[1]
    normed_two = normed_f.astype(bf16)
    logits = jnp.dot(normed_f, w_router, precision=PRECISE, preferred_element_type=f32)

    expert_ids = jnp.arange(EXPERTS, dtype=jnp.int32)
    chosen = jnp.any(routes[:, :, None] == expert_ids[None, None, :], axis=1)
    masked_logits = jnp.where(chosen, logits, NEG_FILL)
    gate_exp = jnp.where(
        chosen, jnp.exp(masked_logits - jnp.max(masked_logits, axis=-1, keepdims=True)), 0.0
    )
    gates = gate_exp / jnp.sum(gate_exp, axis=-1, keepdims=True)

    if whole_experts:
        shared_rows = gather_partners(normed_two, "col")
        shared_grads = gather_partners(cotangent, "col")
        shared_gates = gather_partners(gates, "col")
        shared_routes = gather_partners(routes, "col")
        own_col = jnp.arange(share_count, dtype=jnp.int32) == lax.axis_index("col")
        near_ids = (
            jnp.arange(near_experts, dtype=jnp.int32) * share_count + lax.axis_index("col")
        )
        near_gates = jnp.sum(
            jnp.where(own_col, shared_gates.reshape(-1, near_experts, share_count), 0.0), axis=2
        )
    else:
        shared_rows, shared_grads, shared_routes = normed_two, cotangent, routes
        near_ids, near_gates = expert_ids, gates
    shared_count = shared_rows.shape[0]

    near_chosen = jnp.any(shared_routes[:, :, None] == near_ids[None, None, :], axis=1)
    earlier = jnp.tril(jnp.ones((shared_count, shared_count), bf16), -1)
    ranking = jnp.dot(earlier, near_chosen.astype(bf16), preferred_element_type=f32)
    rank_of = jnp.where(near_chosen, ranking.astype(jnp.int32), -1).T
    slot_ids = jnp.arange(slot_rows, dtype=jnp.int32)
    in_slot = rank_of[:, None, :] == slot_ids[None, :, None]
    slot_count = near_experts * slot_rows
    pick = in_slot.astype(bf16).reshape(slot_count, shared_count)
    slot_gates = jnp.where(in_slot, near_gates.T[:, None, :], 0.0)
    slot_gate = jnp.sum(slot_gates, axis=-1).reshape(slot_count, 1)
    slot_gates = slot_gates.reshape(slot_count, shared_count)
    gates_high = slot_gates.astype(bf16)
    gates_low = (slot_gates - gates_high.astype(f32)).astype(bf16)

    def dispatch(first_rows, second_rows, weights):
        slots = (sources, held_experts, slot_rows, width)
        both = jnp.concatenate([first_rows.reshape(slots), second_rows.reshape(slots)], axis=2)
        both, weights = lax.optimization_barrier((both, weights))
        moved = lax.all_to_all(both, expert_axes, split_axis=0, concat_axis=0, tiled=True)
        moved = jnp.swapaxes(moved, 0, 1)
        held = (held_experts, sources * slot_rows, width)
        return (
            moved[:, :, :slot_rows].reshape(held),
            moved[:, :, slot_rows:].reshape(held),
            weights,
        )

    def bring_back(first_rows, second_rows):
        held = (held_experts, sources, slot_rows, width)
        both = jnp.concatenate([first_rows.reshape(held), second_rows.reshape(held)], axis=2)
        moved = lax.all_to_all(
            jnp.swapaxes(both, 0, 1), expert_axes, split_axis=0, concat_axis=0, tiled=True
        )
        slots = (slot_count, width)
        return (
            moved[:, :, :slot_rows].reshape(slots),
            moved[:, :, slot_rows:].reshape(slots),
        )

    upstream = cotangent.astype(f32)
    received, received_grad, expert_w = dispatch(
        jnp.dot(pick, shared_rows, preferred_element_type=f32).astype(bf16),
        (slot_gate * jnp.dot(pick, shared_grads, preferred_element_type=f32)).astype(bf16),
        expert_w,
    )
    in_w = expert_w[:, :, : 2 * ff]
    down_wt = expert_w[:, :, 2 * ff :]
    pre = jnp.einsum("jrd,jdf->jrf", received, in_w, preferred_element_type=f32)
    gate_pre = pre[:, :, :ff]
    up_pre = pre[:, :, ff:]
    sigm = jax.nn.sigmoid(gate_pre)
    silu_gate = gate_pre * sigm
    hidden_act = (silu_gate * up_pre).astype(bf16)
    act_grad = jnp.einsum("jrd,jdf->jrf", received_grad, down_wt, preferred_element_type=f32)
    silu_slope = sigm * (1.0 + gate_pre * (1.0 - sigm))
    pre_grad = jnp.concatenate(
        [(act_grad * up_pre * silu_slope).astype(bf16), (act_grad * silu_gate).astype(bf16)],
        axis=2,
    )
    returned, returned_grad = bring_back(
        jnp.einsum("jrf,jdf->jrd", hidden_act, down_wt, preferred_element_type=f32).astype(bf16),
        jnp.einsum("jrf,jdf->jrd", pre_grad, in_w, preferred_element_type=f32).astype(bf16),
    )
    in_wgrad = jnp.einsum("jrd,jrf->jdf", received, pre_grad, preferred_element_type=f32)
    down_wtgrad = jnp.einsum(
        "jrd,jrf->jdf", received_grad, hidden_act, preferred_element_type=f32
    )
    expert_wgrad = jnp.concatenate([in_wgrad.astype(bf16), down_wtgrad.astype(bf16)], axis=2)

    expert_wgrad, returned_grad = lax.optimization_barrier((expert_wgrad, returned_grad))
    rows_back = contract_rows(pick, returned_grad)
    all_gate_grads = contract_cols(returned, shared_grads)
    all_gate_grads = all_gate_grads.reshape(near_experts, slot_rows, shared_count)
    gate_grads = jnp.sum(jnp.where(in_slot, all_gate_grads, 0.0), axis=1).T
    moe = contract_rows(gates_high, returned) + contract_rows(gates_low, returned)
    if whole_experts:
        rows_back = sum_partners(rows_back, "col", tok_rows)
        moe = sum_partners(moe, "col", tok_rows)
        wide_grads = jnp.zeros((tok_rows, near_experts, share_count), f32)
        for step in range(share_count):
            part_grads = gate_grads[step * tok_rows : (step + 1) * tok_rows]
            if step:
                part_grads = lax.ppermute(part_grads, "col", partner_list("col", step))
            from_col = jnp.arange(share_count, dtype=jnp.int32) == (lax.axis_index("col") ^ step)
            wide_grads = wide_grads + jnp.where(from_col, part_grads[:, :, None], 0.0)
        gate_grads = wide_grads.reshape(tok_rows, EXPERTS)
    block_out = (hidden + moe).astype(bf16)
    logit_grad = gates * (gate_grads - jnp.sum(gates * gate_grads, axis=-1, keepdims=True))
    router_grad_t = lax.dot_general(
        logit_grad,
        normed_f,
        (((0,), (0,)), ((), ())),
        precision=PRECISE,
        preferred_element_type=f32,
    )
    normed_grad = lax.dot_general(
        logit_grad,
        w_router,
        (((1,), (1,)), ((), ())),
        precision=PRECISE,
        preferred_element_type=f32,
    ) + rows_back
    hidden_norm_grad, gain_two_grad = norm_back(hidden, inverse_two, gains[1], normed_grad)
    hidden_grad = upstream + hidden_norm_grad
    attended_grad = hidden_grad.astype(bf16)
    piece = gather_partners(attended_grad, "col")
    part = jnp.dot(piece, output_wt, preferred_element_type=f32)
    output_wtgrad = contract_rows(piece, mixed_b)
    mixed_grad_b = part.astype(bf16).reshape(att_rows, heads_kv, group_width, HEAD_SIZE)
    scores_again = masked_scores(query_b, keys_b, allowed, scale_factor)
    probs_again = jnp.exp(scores_again - log_total)
    probs_grad = jnp.einsum("qngd,knd->ngqk", mixed_grad_b, values_b, preferred_element_type=f32)
    value_grad = jnp.einsum(
        "ngqk,qngd->knd", probs_again.astype(bf16), mixed_grad_b, preferred_element_type=f32
    )
    inner_sum = jnp.sum(probs_again * probs_grad, axis=-1, keepdims=True)
    score_grad = (probs_again * (probs_grad - inner_sum)).astype(bf16)
    query_grad = (
        jnp.einsum("ngqk,knd->qngd", score_grad, keys_b, preferred_element_type=f32) * scale_factor
    )
    key_grad = (
        jnp.einsum("ngqk,qngd->knd", score_grad, query_b, preferred_element_type=f32) * scale_factor
    )
    query_lin_grad = (
        unrotate(query_grad.reshape(att_rows, heads_q, HEAD_SIZE), cosine_lookup, sine_lookup)
        .astype(bf16)
        .reshape(att_rows, q_cols)
    )
    key_lin_grad = (
        unrotate(key_grad, cosine_lookup, sine_lookup).astype(bf16).reshape(att_rows, kv_cols)
    )
    value_lin_grad = value_grad.astype(bf16).reshape(att_rows, kv_cols)
    joint_grad = jnp.concatenate([query_lin_grad, key_lin_grad, value_lin_grad], axis=1)
    shared_grad = contract_cols(joint_grad, joint_w)
    gain_one_grad = jnp.sum(shared_grad * block_rows.astype(f32), axis=0) / gains[0]
    normed_one_grad = sum_partners(shared_grad, "col", tok_rows)
    joint_wgrad = contract_rows(block_rows, joint_grad)
    tokens_norm_grad, _ = norm_back(tokens_f, inverse_one, gains[0], normed_one_grad)
    tokens_grad = hidden_grad + tokens_norm_grad

    if whole_experts:
        expert_g = lax.all_to_all(
            expert_wgrad.reshape(group_count, width // group_count, 3 * ff),
            ("row", "col"),
            split_axis=0,
            concat_axis=0,
            tiled=True,
        )
    else:
        expert_g = lax.psum_scatter(
            expert_wgrad, ("row", "col"), scatter_dimension=1, tiled=True
        )
    attention_wgrad = jnp.concatenate(
        [joint_wgrad.astype(bf16), output_wtgrad.astype(bf16)], axis=1
    )
    attention_wgrad, expert_g = lax.optimization_barrier((attention_wgrad, expert_g))
    expert_g = expert_g.astype(f32)
    attention_g = exchange_sum(attention_wgrad, ("dp", "row"), owner_count)
    query_g = attention_g[:, :q_cols]
    key_g = attention_g[:, q_cols : q_cols + kv_cols]
    value_g = attention_g[:, q_cols + kv_cols : joint_cols]
    output_g = attention_g[:, joint_cols:].T
    gate_g = expert_g[:, :, :ff]
    up_g = expert_g[:, :, ff : 2 * ff]
    down_g = jnp.swapaxes(expert_g[:, :, 2 * ff :], 1, 2)
    small_total = sum_all(
        jnp.concatenate([gain_one_grad[None], gain_two_grad[None], router_grad_t], axis=0),
        ("dp", "row", "col"),
    )
    gains_total = small_total[:2]
    router_total = small_total[2:].T
    gains_out = adam_update(gains, gains_total, gains_first, gains_second, GAIN_RATE, 0.0)
    query_out = adam_update(w_query, query_g, query_first, query_second, LEARN_RATE, WEIGHT_DECAY)
    key_out = adam_update(w_key, key_g, key_first, key_second, LEARN_RATE, WEIGHT_DECAY)
    value_out = adam_update(w_value, value_g, value_first, value_second, LEARN_RATE, WEIGHT_DECAY)
    output_out = adam_update(
        w_output, output_g, output_first, output_second, LEARN_RATE, WEIGHT_DECAY
    )
    router_out = adam_update(
        w_router, router_total, router_first, router_second, LEARN_RATE, WEIGHT_DECAY
    )
    gate_out = adam_update(w_gate, gate_g, gate_first, gate_second, LEARN_RATE, WEIGHT_DECAY)
    up_out = adam_update(w_up, up_g, up_first, up_second, LEARN_RATE, WEIGHT_DECAY)
    down_out = adam_update(w_down, down_g, down_first, down_second, LEARN_RATE, WEIGHT_DECAY)
    return (
        block_out,
        tokens_grad,
        gains_out[0],
        gains_out[1],
        gains_out[2],
        query_out[0],
        query_out[1],
        query_out[2],
        key_out[0],
        key_out[1],
        key_out[2],
        value_out[0],
        value_out[1],
        value_out[2],
        output_out[0],
        output_out[1],
        output_out[2],
        router_out[0],
        router_out[1],
        router_out[2],
        gate_out[0],
        gate_out[1],
        gate_out[2],
        up_out[0],
        up_out[1],
        up_out[2],
        down_out[0],
        down_out[1],
        down_out[2],
    )


def solution(mesh):
    placed = (
        P(("dp", "row", "col"), None),
        P(("dp", "row", "col"), None),
        P(("dp", "row"), None),
        P(("dp", "row", "col"), None),
        P(),
        P(),
        P(),
        P(("dp", "row"), "col"),
        P(("dp", "row"), "col"),
        P(("dp", "row"), "col"),
        P(("dp", "row"), "col"),
        P(("dp", "row"), "col"),
        P(("dp", "row"), "col"),
        P(("dp", "row"), "col"),
        P(("dp", "row"), "col"),
        P(("dp", "row"), "col"),
        P("col", ("dp", "row")),
        P("col", ("dp", "row")),
        P("col", ("dp", "row")),
        P(),
        P(),
        P(),
        P("dp", ("row", "col"), None),
        P("dp", ("row", "col"), None),
        P("dp", ("row", "col"), None),
        P("dp", ("row", "col"), None),
        P("dp", ("row", "col"), None),
        P("dp", ("row", "col"), None),
        P("dp", None, ("row", "col")),
        P("dp", None, ("row", "col")),
        P("dp", None, ("row", "col")),
    )
    return jax.shard_map(
        on_device,
        mesh=mesh,
        in_specs=placed,
        out_specs=(
            P(("dp", "row", "col"), None),
            P(("dp", "row", "col"), None),
            P(),
            P(),
            P(),
            P(("dp", "row"), "col"),
            P(("dp", "row"), "col"),
            P(("dp", "row"), "col"),
            P(("dp", "row"), "col"),
            P(("dp", "row"), "col"),
            P(("dp", "row"), "col"),
            P(("dp", "row"), "col"),
            P(("dp", "row"), "col"),
            P(("dp", "row"), "col"),
            P("col", ("dp", "row")),
            P("col", ("dp", "row")),
            P("col", ("dp", "row")),
            P(),
            P(),
            P(),
            P("dp", ("row", "col"), None),
            P("dp", ("row", "col"), None),
            P("dp", ("row", "col"), None),
            P("dp", ("row", "col"), None),
            P("dp", ("row", "col"), None),
            P("dp", ("row", "col"), None),
            P("dp", None, ("row", "col")),
            P("dp", None, ("row", "col")),
            P("dp", None, ("row", "col")),
        ),
        check_vma=False,
    )
```
